256 devices in a mesh: seqhi: 16 (over y, x_lo, core), seqlo: 16 (over x_hi, z).
Axes of the slice: x: 4 (x_hi: 2, x_lo: 2; x = x_hi * 2 + x_lo), y: 4, z: 8, core: 2. Of those that a mesh axis runs over, the one named last changes fastest.
Arguments:
- tokens: bfloat16 [262144, 768], P(('seqhi', 'seqlo')), may hold values from -24 to 24
- cotangent: bfloat16 [262144, 768], P(('seqhi', 'seqlo')), may hold values from -24 to 24
- first_kernel_weight: bfloat16 [2304, 384], replicated, may hold values from -0.125 to 0.125
- first_pointwise_weight: bfloat16 [768, 384], replicated, may hold values from -0.3125 to 0.3125
- second_kernel_weight: bfloat16 [2304, 384], replicated, may hold values from -0.125 to 0.125
- second_pointwise_weight: bfloat16 [768, 384], replicated, may hold values from -0.3125 to 0.3125
Outputs:
- output: bfloat16 [262144, 768], P(('seqhi', 'seqlo'))
- token_rows_gradient: bfloat16 [262144, 768], P(('seqhi', 'seqlo'))
- first_kernel_gradient: float32 [2304, 384], P(('seqhi', 'seqlo'))
- first_pointwise_gradient: float32 [768, 384], P(('seqhi', 'seqlo'))
- second_kernel_gradient: float32 [2304, 384], P(('seqhi', 'seqlo'))
- second_pointwise_gradient: float32 [768, 384], P(('seqhi', 'seqlo'))
The draws below stay inside these ranges and needn't reach their ends.
All inputs are finite; a program needn't handle non-finite values.
Results may differ from the reference program's by a relative error of at most 0.015.
Values may be sent and summed in bfloat16 or wider, within the bound.
No kernel may reach another device: no remote copies, remote signals or barrier semaphores. Data moves between devices by JAX's collectives and lax.ppermute only.
A program may use at most 128 MiB of HBM per device.

```python
import jax
import jax.numpy as jnp

D = 768
H = 384
TAPS = 3
BINS = 262144
FIRST_SPACING = 4096
SECOND_SPACING = 8192


def with_spikes(drawn, key, source, target, parts, factor):
    owner, partner = [(jnp.arange(drawn.shape[dim]) // (drawn.shape[dim] // parts)).reshape([-1 if axis == dim else 1 for axis in range(drawn.ndim)]) for dim in (source, target)]
    chosen = jax.random.permutation(key, parts)[partner]
    strong = (owner == chosen) | (owner == (partner + parts // 2) % parts)
    return jnp.where(strong, factor * drawn, drawn)


def steps_of(stream_key, extent, cuts, least, high):
    factor_of, own = 1.0, jax.random.fold_in(stream_key, 6)
    for dim, blocks in cuts:
        steps = jnp.exp(jax.random.uniform(jax.random.fold_in(own, dim), (blocks,), jnp.float32, least / len(cuts), high / len(cuts)))
        factor_of = factor_of * jnp.repeat(steps, extent[dim] // blocks).reshape([-1 if axis == dim else 1 for axis in range(len(extent))])
    return factor_of


def bell_draw(stream_key, dims, width, limit, pieces=(), kind=jnp.bfloat16):
    factor_of = steps_of(stream_key, dims, pieces, -0.22, 0.18) if pieces else 1.0
    entries = jax.random.normal(stream_key, dims, jnp.float32) * width * factor_of
    return jnp.minimum(jnp.maximum(entries, -limit), limit).astype(kind)


def heavy_noise(rng, shape, width, reach, split, heavy, held_as=jnp.bfloat16):
    values = width * jax.random.normal(rng, shape, jnp.float32)
    if split:
        values = values * steps_of(rng, shape, split, -0.22, 0.18)
    return jnp.clip(with_spikes(values, jax.random.fold_in(rng, 3), *heavy), -reach, reach).astype(held_as)


def setup_inputs(seed: int = 0) -> dict:
    arg_keys = jax.random.split(jax.random.key(seed), 7)
    tokens = heavy_noise(arg_keys[0], (BINS, D), 1.0, 24.0, ((0, 256),), (0, 1, 256, 6.0))
    cotangent = heavy_noise(arg_keys[1], (BINS, D), 1.0, 24.0, ((0, 256),), (0, 1, 256, 6.0))
    first_kernel_weight = bell_draw(arg_keys[2], (TAPS * D, H), (TAPS * D) ** -0.5, 0.125)
    first_pointwise_weight = bell_draw(arg_keys[3], (D, H), H ** -0.5, 0.3125)
    second_kernel_weight = bell_draw(arg_keys[4], (TAPS * D, H), (TAPS * D) ** -0.5, 0.125)
    second_pointwise_weight = bell_draw(arg_keys[5], (D, H), H ** -0.5, 0.3125)
    return dict(tokens=tokens, cotangent=cotangent, first_kernel_weight=first_kernel_weight, first_pointwise_weight=first_pointwise_weight, second_kernel_weight=second_kernel_weight, second_pointwise_weight=second_pointwise_weight)


def shifted(values, offset):
    padding = jnp.zeros((abs(offset), values.shape[1]), values.dtype)
    if offset > 0:
        return jnp.concatenate([values[offset:], padding], 0)
    return jnp.concatenate([padding, values[:offset]], 0)

def tap_inputs(tokens, dilation):
    return (shifted(tokens, -dilation), tokens, shifted(tokens, dilation))

def residual_block_forward(tokens, conv_weight, proj_weight, dilation):
    tap_rows = tap_inputs(tokens, dilation)
    pre = jnp.zeros((tokens.shape[0], H), jnp.float32)
    for tap_index in range(TAPS):
        pre = pre + jnp.dot(tap_rows[tap_index], conv_weight[tap_index * D:(tap_index + 1) * D], preferred_element_type=jnp.float32)
    inner = jax.nn.gelu(pre).astype(jnp.bfloat16)
    result = (tokens.astype(jnp.float32) + jnp.dot(inner, proj_weight.T, preferred_element_type=jnp.float32)).astype(jnp.bfloat16)
    return (result, pre, inner)

def residual_block_backward(grad_out, tokens, pre, inner, conv_weight, proj_weight, dilation):
    grad_proj = jnp.dot(grad_out.T, inner, preferred_element_type=jnp.float32)
    grad_inner = jnp.dot(grad_out, proj_weight, preferred_element_type=jnp.float32)
    _, pullback = jax.vjp(jax.nn.gelu, pre)
    grad_pre = pullback(grad_inner)[0].astype(jnp.bfloat16)
    tap_rows = tap_inputs(tokens, dilation)
    grad_conv = jnp.concatenate([jnp.dot(tap_rows[tap_index].T, grad_pre, preferred_element_type=jnp.float32) for tap_index in range(TAPS)], 0)
    moved = (shifted(grad_pre, dilation), grad_pre, shifted(grad_pre, -dilation))
    grad_in = grad_out.astype(jnp.float32)
    for tap_index in range(TAPS):
        grad_in = grad_in + jnp.dot(moved[tap_index], conv_weight[tap_index * D:(tap_index + 1) * D].T, preferred_element_type=jnp.float32)
    return (grad_in.astype(jnp.bfloat16), grad_conv, grad_proj)

def reference(tokens, cotangent, first_kernel_weight, first_pointwise_weight, second_kernel_weight, second_pointwise_weight):
    between_blocks_state, first_preactivation, first_hidden_state = residual_block_forward(tokens, first_kernel_weight, first_pointwise_weight, FIRST_SPACING)
    output, second_preactivation, second_hidden_state = residual_block_forward(between_blocks_state, second_kernel_weight, second_pointwise_weight, SECOND_SPACING)
    between_blocks_gradient, second_kernel_gradient, second_pointwise_gradient = residual_block_backward(cotangent, between_blocks_state, second_preactivation, second_hidden_state, second_kernel_weight, second_pointwise_weight, SECOND_SPACING)
    token_rows_gradient, first_kernel_gradient, first_pointwise_gradient = residual_block_backward(between_blocks_gradient, tokens, first_preactivation, first_hidden_state, first_kernel_weight, first_pointwise_weight, FIRST_SPACING)
    return (output, token_rows_gradient, first_kernel_gradient, first_pointwise_gradient, second_kernel_gradient, second_pointwise_gradient)
```

```python
import jax
import jax.numpy as jnp
from jax import lax
from jax.sharding import Mesh
from jax.sharding import PartitionSpec as P

AXES = ("y", "x_lo", "core", "x_hi", "z")
FINE_SHAPE = (4, 2, 2, 2, 8)
FIRST_SPACING = 4096
SECOND_SPACING = 8192
CHUNKS = 2
D = 768


def permuted(x, target):
    devices = 256
    pairs = [(i, target(i)) for i in range(devices) if 0 <= target(i) < devices]
    return lax.ppermute(x, AXES, pairs)


def across(x, reach):
    return permuted(x, lambda i: i ^ reach)


def toward_own_parity(x, reach, sign):
    return permuted(x, lambda i: i + (sign if i & reach else -sign) * 2 * reach)


def dot(a, b):
    return jnp.dot(a, b, preferred_element_type=jnp.float32)


def dot_t(a, b):
    return lax.dot_general(a, b, (((1,), (1,)), ((), ())), preferred_element_type=jnp.float32)


def contract_rows(a, b):
    return lax.dot_general(a, b, (((0,), (0,)), ((), ())), preferred_element_type=jnp.float32)


def bf16(x):
    return x.astype(jnp.bfloat16)


class Block:
    def __init__(self, index, kernel_weight, proj_weight, reach):
        self.reach = reach
        self.even = (index // reach) % 2 == 0
        first, self.center, last = (kernel_weight[k * D : (k + 1) * D] for k in range(3))
        self.near = jnp.where(self.even, first, last)
        self.far = jnp.where(self.even, last, first)
        self.proj = proj_weight

    def forward_sum(self, x):
        sent = bf16(dot(x, self.far))
        arrived = toward_own_parity(sent, self.reach, 1)
        partial = bf16(dot(x, self.near) + arrived.astype(jnp.float32))
        return across(partial, self.reach)

    def forward(self, x):
        pre = dot(x, self.center) + self.forward_sum(x).astype(jnp.float32)
        inner = bf16(jax.nn.gelu(pre))
        out = bf16(x.astype(jnp.float32) + dot_t(inner, self.proj))
        return out, pre, inner

    def backward(self, g, pre):
        grad_inner = dot(g, self.proj)
        _, pullback = jax.vjp(jax.nn.gelu, pre)
        own = bf16(pullback(grad_inner)[0])
        near = across(own, self.reach)
        far = toward_own_parity(near, self.reach, -1)
        gx = bf16(
            g.astype(jnp.float32)
            + dot_t(own, self.center)
            + dot_t(near, self.near)
            + dot_t(far, self.far)
        )
        return gx, own, near, far


def summed(terms):
    total = terms[0]
    for term in terms[1:]:
        total = total + term
    return total


def plane_sum(partials, core):
    n = len(partials)
    stack = jnp.stack([bf16(p).reshape(8, 2, 48, 384) for p in partials], 1)
    kept = lax.dynamic_index_in_dim(stack, core, 2, keepdims=False)
    given = lax.dynamic_index_in_dim(stack, 1 - core, 2, keepdims=False)
    arrived = across(given, 16)
    pair = bf16(kept.astype(jnp.float32) + arrived.astype(jnp.float32))
    pieces = lax.all_to_all(pair, ("y", "x_lo"), 0, 0, tiled=True)
    return jnp.sum(pieces.astype(jnp.float32), 0)


def line_sum(rows):
    n = rows.shape[0]
    pieces = bf16(rows).reshape(n, 16, 3 * 384).swapaxes(0, 1)
    pieces = lax.all_to_all(pieces, ("x_hi", "z"), 0, 0, tiled=True)
    return jnp.sum(pieces.astype(jnp.float32), 0)


def by_tap(even, near, center, far):
    return [jnp.where(even, near, far), center, jnp.where(even, far, near)]


def owned_rows(index, taps):
    taps = jnp.stack(taps)
    parts = []
    for slot in range(3):
        mine = lax.dynamic_index_in_dim(taps, (slot + 2 * index) % 3, 0, keepdims=False)
        targets = {(3 * d + slot) % 256: d for d in range(256)}
        parts.append(permuted(mine, lambda i: targets[i]))
    return jnp.concatenate([p.reshape(3, 384) for p in parts], 0)


def per_device(x, cotangent, w1, p1, w2, p2):
    index = lax.axis_index(AXES)
    core = lax.axis_index("core")
    rows = x.shape[0]
    first = Block(index, w1, p1, FIRST_SPACING // rows)
    second = Block(index, w2, p2, SECOND_SPACING // rows)
    size = rows // CHUNKS
    xs = [x[i * size : (i + 1) * size] for i in range(CHUNKS)]
    gs = [cotangent[i * size : (i + 1) * size] for i in range(CHUNKS)]
    outputs, gxs = [], []
    early, middle, late = [], [], []
    for x, g in zip(xs, gs):
        mid, pre1, inner1 = first.forward(x)
        out, pre2, inner2 = second.forward(mid)
        gmid, own2, near2, far2 = second.backward(g, pre2)
        gx, own1, near1, far1 = first.backward(gmid, pre1)
        outputs.append(out)
        gxs.append(gx)
        early.append(
            [
                contract_rows(g, inner2),
                contract_rows(mid, own2),
                contract_rows(mid, near2),
                contract_rows(mid, far2),
                contract_rows(gmid, inner1),
            ]
        )
        middle.append([contract_rows(x, own1), contract_rows(x, near1)])
        late.append([contract_rows(x, far1)])
    early, middle, late = (
        [summed(t) for t in zip(*group)] for group in (early, middle, late)
    )
    early, middle, late = (plane_sum(group, core) for group in (early, middle, late))
    taps1 = by_tap(first.even, middle[1], middle[0], late[0])
    taps2 = by_tap(second.even, early[2], early[1], early[3])
    done2 = line_sum(jnp.stack([early[0], early[4]] + taps2))
    done1 = line_sum(jnp.stack(taps1))
    return (
        jnp.concatenate(outputs, 0),
        jnp.concatenate(gxs, 0),
        owned_rows(index, [done1[0], done1[1], done1[2]]),
        done2[1].reshape(3, 384),
        owned_rows(index, [done2[2], done2[3], done2[4]]),
        done2[0].reshape(3, 384),
    )


def solution(mesh):
    fine = Mesh(mesh.devices.reshape(FINE_SHAPE), AXES)
    placed = P(AXES, None)
    return jax.shard_map(
        per_device,
        mesh=fine,
        in_specs=(placed, placed, P(), P(), P(), P()),
        out_specs=(placed,) * 6,
        check_vma=False,
    )
```

```python
import functools

import jax
import jax.numpy as jnp
from jax import lax
from jax.experimental import pallas as pl
from jax.experimental.pallas import tpu as pltpu
from jax.sharding import Mesh
from jax.sharding import PartitionSpec as P

AXES = ("y", "x_lo", "core", "x_hi", "z")
FINE_SHAPE = (4, 2, 2, 2, 8)
DEVICES = 256
FIRST_SPACING = 4096
SECOND_SPACING = 8192
CHUNKS = 2
TILE = 256
D = 768
H = 384
EARLY_AFTER = 1
UNIT = 48
F32 = jnp.float32
BF16 = jnp.bfloat16
FAR1, NEAR1, FAR2, NEAR2, CORE, PLANE = range(6)


def permuted(x, target):
    pairs = [(i, target(i)) for i in range(DEVICES) if 0 <= target(i) < DEVICES]
    return lax.ppermute(x, AXES, pairs)


def across(x, reach):
    return permuted(x, lambda i: i ^ reach)


def within_parity(x, reach, sign):
    return permuted(x, lambda i: i + (sign if i & reach else -sign) * 2 * reach)


def dot(a, b):
    return jnp.dot(a, b, preferred_element_type=F32)


def dot_t(a, b):
    return lax.dot_general(a, b, (((1,), (1,)), ((), ())), preferred_element_type=F32)


def contract_rows(a, b):
    return lax.dot_general(a, b, (((0,), (0,)), ((), ())), preferred_element_type=F32)


def gelu_terms(v):
    slope = 0.7978845608028654
    t = jnp.tanh(slope * (v + 0.044715 * (v * v * v)))
    half = 0.5 * (1.0 + t)
    value = v * half
    derivative = half + 0.5 * v * (1.0 - t * t) * (slope * (1.0 + 0.134145 * (v * v)))
    return value, derivative


def row_block(width, first=0):
    return pl.BlockSpec((TILE, width), lambda i, s: (i + first, 0))


def tap(place):
    return pl.BlockSpec((D, H), lambda i, s: (s[place], 0))


CENTER = pl.BlockSpec((D, H), lambda i, s: (1, 0))
WHOLE = pl.BlockSpec((D, H), lambda i, s: (0, 0))
ANYWHERE = pl.BlockSpec(memory_space=pl.ANY)
IN_VMEM = pl.BlockSpec(memory_space=pltpu.VMEM)

SHORT = pl.CostEstimate(flops=1, bytes_accessed=1, transcendentals=0)


def into_rows(body, scalars, chunk, rows, operands, name, previous):
    n = len(operands)
    tiles = rows // CHUNKS // TILE

    def wrapped(s, *refs):
        body(s, *refs[:n], refs[-1])

    return pl.pallas_call(
        wrapped,
        out_shape=jax.ShapeDtypeStruct((rows, D), BF16),
        grid_spec=pltpu.PrefetchScalarGridSpec(
            num_scalar_prefetch=1,
            grid=(tiles,),
            in_specs=[spec for _, spec in operands] + [ANYWHERE] * len(previous),
            out_specs=row_block(D, chunk * tiles),
        ),
        cost_estimate=SHORT,
        compiler_params=pltpu.CompilerParams(vmem_limit_bytes=24 * 2**20),
        input_output_aliases={1 + n: 0} if previous else {},
        name=name,
    )(scalars, *[a for a, _ in operands], *previous)


def resident(body, name, scalars, operands, outs, after=(), vmem=8):
    n = len(operands)

    def wrapped(s, *refs):
        body(s, *refs[:n], *refs[n + len(after) :])

    return pl.pallas_call(
        wrapped,
        out_shape=[jax.ShapeDtypeStruct(shape, BF16) for shape in outs],
        in_specs=[pl.BlockSpec(memory_space=pltpu.SMEM)] + [IN_VMEM] * n + [ANYWHERE] * len(after),
        out_specs=[IN_VMEM] * len(outs),
        cost_estimate=SHORT,
        compiler_params=pltpu.CompilerParams(vmem_limit_bytes=vmem * 2**20),
        name=name,
    )(scalars, *operands, *after)


def tap_of(s, weight, place):
    return weight[pl.ds(pl.multiple_of(s[place] * D, D), D), :]


def center_of(weight):
    return weight[D : 2 * D, :]


def tiles_of(ref):
    return [slice(i, i + TILE) for i in range(0, ref.shape[0], TILE)]


def from_row(first, rows):
    return slice(first + rows.start, first + rows.stop)


def first_product(s, x, w_far, sent):
    sent[...] = dot(x[...], w_far[...]).astype(BF16)


def near_sum(s, x, weight, arrived, total, place, first=0):
    w = tap_of(s, weight, place)
    for r in tiles_of(total):
        total[r] = (dot(x[from_row(first, r)], w) + arrived[r].astype(F32)).astype(BF16)


def first_block(s, x, crossed, w1, proj, w2, mid, inner, slope, sent, first):
    w_center, w_far2 = center_of(w1), tap_of(s, w2, FAR2)
    for r in tiles_of(mid):
        rows = x[from_row(first, r)]
        value, derivative = gelu_terms(dot(rows, w_center) + crossed[r].astype(F32))
        slope[r] = derivative.astype(BF16)
        value = value.astype(BF16)
        inner[r] = value
        result = (rows.astype(F32) + dot_t(value, proj[...])).astype(BF16)
        mid[r] = result
        sent[r] = dot(result, w_far2).astype(BF16)


def second_block(s, mid, crossed, w2, g, proj, own, inner, first):
    w_center = center_of(w2)
    for r in tiles_of(mid):
        value, derivative = gelu_terms(dot(mid[r], w_center) + crossed[r].astype(F32))
        inner[r] = value.astype(BF16)
        own[r] = (derivative * dot(g[from_row(first, r)], proj[...])).astype(BF16)


def input_gradient(g, own, near, far, w_center, w_near, w_far):
    return (
        g.astype(F32) + dot_t(own, w_center) + dot_t(near, w_near) + dot_t(far, w_far)
    ).astype(BF16)


def middle_gradient(s, g, own, near, far, w2, proj, slope, gmid, own1, first):
    taps = center_of(w2), tap_of(s, w2, NEAR2), tap_of(s, w2, FAR2)
    for r in tiles_of(gmid):
        result = input_gradient(g[from_row(first, r)], own[r], near[r], far[r], *taps)
        gmid[r] = result
        own1[r] = (slope[r].astype(F32) * dot(result, proj[...])).astype(BF16)


def output_rows(s, mid, inner2, proj, out):
    out[...] = (mid[...].astype(F32) + dot_t(inner2[...], proj[...])).astype(BF16)


def gradient_rows(s, gmid, own, near, far, w_center, w_near, w_far, gx):
    gx[...] = input_gradient(
        gmid[...], own[...], near[...], far[...], w_center[...], w_near[...], w_far[...]
    )


def place_rows(s, total, kept, given, block_rows, unit_of, row_in_block):
    for i in range(total.shape[0] // UNIT):
        block, offset = unit_of(i)
        row = (block // 2) * block_rows + row_in_block + offset * UNIT
        row = row if isinstance(row, int) else pl.multiple_of(row, UNIT)
        piece = total[i * UNIT : (i + 1) * UNIT].astype(BF16)

        @pl.when(block % 2 == s[CORE])
        def _():
            kept[pl.ds(row, UNIT), :] = piece

        @pl.when(block % 2 != s[CORE])
        def _():
            given[pl.ds(row, UNIT), :] = piece


def kernel_gradient(s, xs, owns, nears, fars, near_place, far_place, kept, given, block_rows):
    for half in range(2):
        columns = slice(half * 384, half * 384 + 384)
        total = sum(
            contract_rows(x[:, columns], jnp.concatenate([o[...], n[...], f[...]], 1))
            for x, o, n, f in zip(xs, owns, nears, fars)
        )
        for j, k in enumerate((1, s[near_place], s[far_place])):

            def unit_of(i, k=k):
                u = k * 16 + half * 8 + i
                return u // 3, u % 3

            place_rows(s, total[:, j * H : (j + 1) * H], kept, given, block_rows, unit_of, 0)


def by_chunk(ref):
    size = ref.shape[0] // CHUNKS
    return [ref.at[pl.ds(c * size, size)] for c in range(CHUNKS)]


def early_gradients(s, g, *refs):
    kept, given = refs[-2:]
    mids, owns, nears, fars, inner2s, gmids, inner1s = (
        refs[i * CHUNKS : (i + 1) * CHUNKS] for i in range(7)
    )
    kernel_gradient(s, mids, owns, nears, fars, NEAR2, FAR2, kept, given, 240)
    for lefts, rights, first_row in ((by_chunk(g), inner2s, 144), (gmids, inner1s, 192)):
        for half in range(2):
            columns = slice(half * 384, half * 384 + 384)
            total = sum(contract_rows(a[:, columns], b[...]) for a, b in zip(lefts, rights))
            place_rows(
                s, total, kept, given, 240, lambda i, half=half: (half * 8 + i, 0), first_row
            )


def late_gradients(s, x, *refs):
    kept, given = refs[-2:]
    owns, nears, fars = (refs[i * CHUNKS : (i + 1) * CHUNKS] for i in range(3))
    kernel_gradient(s, by_chunk(x), owns, nears, fars, NEAR1, FAR1, kept, given, 144)


def add_pair(s, kept, arrived, *pieces):
    rows = pieces[0].shape[0]
    for j, piece in enumerate(pieces):
        place = pl.ds(pl.multiple_of((s[PLANE] ^ j) * rows, UNIT), rows)
        piece[...] = (kept[place, :].astype(F32) + arrived[place, :].astype(F32)).astype(BF16)


def plane_pieces(scalars, kept, given, name):
    arrived = across(given, 16)
    pieces = resident(add_pair, name, scalars, [kept, arrived], [(kept.shape[0] // 8, H)] * 8)
    return [pieces[0]] + [across(pieces[j], 32 * j) for j in range(1, 8)]


def plane_exchange(kept, given):
    arrived = across(given, 16)
    pair = (kept.astype(F32) + arrived.astype(F32)).astype(BF16)
    return lax.all_to_all(pair, ("y", "x_lo"), 0, 0, tiled=True), pair


def sum_pieces(pieces):
    return sum(p[...].astype(F32) for p in pieces)


def arrange_lines(*refs):
    early, late, lines = refs[0], refs[1:9], refs[-1]
    early_rows = sum_pieces(early.at[pl.ds(240 * i, 240)] for i in range(8))
    late_rows = sum_pieces(late)
    for i in range(16):
        lines[i, 0:9] = early_rows[9 * i : 9 * i + 9].astype(BF16)
        lines[i, 9:18] = late_rows[9 * i : 9 * i + 9].astype(BF16)
        lines[i, 18:21] = early_rows[144 + 3 * i : 147 + 3 * i].astype(BF16)
        lines[i, 21:24] = early_rows[192 + 3 * i : 195 + 3 * i].astype(BF16)


def finish(lines, kernel2, kernel1, point2, point1):
    done = jnp.sum(lines[...].astype(F32), 0)
    kernel2[...] = done[0:9]
    kernel1[...] = done[9:18]
    point2[...] = done[18:21]
    point1[...] = done[21:24]


def per_device(x, cotangent, w1, p1, w2, p2):
    index = lax.axis_index(AXES)
    core = lax.axis_index("core")
    rows = x.shape[0]
    reach1, reach2 = FIRST_SPACING // rows, SECOND_SPACING // rows
    odd1, odd2 = (index // reach1) % 2, (index // reach2) % 2
    scalars = jnp.stack([2 - 2 * odd1, 2 * odd1, 2 - 2 * odd2, 2 * odd2, core, index // 32]).astype(
        jnp.int32
    )
    size = rows // CHUNKS
    narrow, wide = (size, H), (size, D)
    chunks = []
    for c in range(CHUNKS):
        here = functools.partial(functools.partial, first=c * size)
        sent = pl.pallas_call(
            first_product,
            out_shape=jax.ShapeDtypeStruct(narrow, BF16),
            grid_spec=pltpu.PrefetchScalarGridSpec(
                num_scalar_prefetch=1,
                grid=(size // TILE,),
                in_specs=[row_block(D, c * (size // TILE)), tap(FAR1)],
                out_specs=row_block(H),
            ),
            cost_estimate=SHORT,
            compiler_params=pltpu.CompilerParams(vmem_limit_bytes=24 * 2**20),
            name="first_product",
        )(scalars, x, w1)
        arrived = within_parity(sent, reach1, 1)
        (total,) = resident(
            here(near_sum, place=NEAR1), "first_near_sum", scalars, [x, w1, arrived], [narrow]
        )
        crossed = across(total, reach1)
        mid, inner1, slope1, sent = resident(
            here(first_block), "first_block", scalars, [x, crossed, w1, p1, w2], [wide] + [narrow] * 3
        )
        arrived = within_parity(sent, reach2, 1)
        (total,) = resident(
            functools.partial(near_sum, place=NEAR2),
            "second_near_sum",
            scalars,
            [mid, w2, arrived],
            [narrow],
        )
        crossed = across(total, reach2)
        own2, inner2 = resident(
            here(second_block), "second_block", scalars, [mid, crossed, w2, cotangent, p2], [narrow] * 2
        )
        near2 = across(own2, reach2)
        far2 = within_parity(near2, reach2, -1)
        gmid, own1 = resident(
            here(middle_gradient),
            "middle_gradient",
            scalars,
            [cotangent, own2, near2, far2, w2, p1, slope1],
            [wide, narrow],
        )
        near1 = across(own1, reach1)
        far1 = within_parity(near1, reach1, -1)
        chunks.append(
            dict(
                mid=mid, inner1=inner1, inner2=inner2, gmid=gmid,
                own1=own1, near1=near1, far1=far1, own2=own2, near2=near2, far2=far2,
            )
        )

    def parts(*names):
        return [chunk[name] for name in names for chunk in chunks]

    kept, given = resident(
        early_gradients,
        "early_gradients",
        scalars,
        [cotangent] + parts("mid", "own2", "near2", "far2", "inner2", "gmid", "inner1"),
        [(8 * 240, H)] * 2,
        after=(chunks[EARLY_AFTER]["near1"],),
        vmem=16,
    )
    early, early_pair = plane_exchange(kept, given)
    kept, given = resident(
        late_gradients,
        "late_gradients",
        scalars,
        [x] + parts("own1", "near1", "far1"),
        [(8 * 144, H)] * 2,
        after=(early_pair,),
        vmem=16,
    )
    late = plane_pieces(scalars, kept, given, "late_pair")

    wide, narrow = row_block(D), row_block(H)
    output, gx = [], []
    for c, chunk in enumerate(chunks):
        whole_rows = functools.partial(into_rows, scalars=scalars, chunk=c, rows=rows)
        output = [
            whole_rows(
                output_rows,
                operands=[(chunk["mid"], wide), (chunk["inner2"], narrow), (p2, WHOLE)],
                name="output_rows",
                previous=output,
            )
        ]
        gx = [
            whole_rows(
                gradient_rows,
                operands=[
                    (chunk["gmid"], wide),
                    (chunk["own1"], narrow),
                    (chunk["near1"], narrow),
                    (chunk["far1"], narrow),
                    (w1, CENTER),
                    (w1, tap(NEAR1)),
                    (w1, tap(FAR1)),
                ],
                name="gradient_rows",
                previous=gx,
            )
        ]
    lines = pl.pallas_call(
        arrange_lines,
        out_shape=jax.ShapeDtypeStruct((16, 24, H), BF16),
        in_specs=[IN_VMEM] * 9,
        out_specs=IN_VMEM,
        cost_estimate=SHORT,
        name="arrange_lines",
    )(early, *late)
    lines = lax.all_to_all(lines, ("x_hi", "z"), 0, 0, tiled=True)
    kernel2, kernel1, point2, point1 = pl.pallas_call(
        finish,
        out_shape=[jax.ShapeDtypeStruct((n, H), F32) for n in (9, 9, 3, 3)],
        in_specs=[IN_VMEM],
        out_specs=[IN_VMEM] * 4,
        cost_estimate=SHORT,
        name="finish",
    )(lines)
    return (output[0], gx[0], kernel1, point1, kernel2, point2)


def solution(mesh):
    fine = Mesh(mesh.devices.reshape(FINE_SHAPE), AXES)
    placed = P(AXES, None)
    return jax.shard_map(
        per_device,
        mesh=fine,
        in_specs=(placed, placed, P(), P(), P(), P()),
        out_specs=(placed,) * 6,
        check_vma=False,
    )
```

```python
import functools

import jax
import jax.numpy as jnp
from jax import lax
from jax.experimental import pallas as pl
from jax.experimental.pallas import tpu as pltpu
from jax.sharding import Mesh
from jax.sharding import PartitionSpec as P

AXES = ("y", "x_lo", "core", "x_hi", "z")
FINE_SHAPE = (4, 2, 2, 2, 8)
DEVICES = 256
FIRST_SPACING = 4096
SECOND_SPACING = 8192
CHUNKS = 2
TILE = 256
D = 768
H = 384
PIECE_ORDER = (4, 5, 6, 7, 2, 3, 1)
UNIT = 48
F32 = jnp.float32
BF16 = jnp.bfloat16
FAR1, NEAR1, FAR2, NEAR2, CORE, PLANE = range(6)


def permuted(x, target):
    pairs = [(i, target(i)) for i in range(DEVICES) if 0 <= target(i) < DEVICES]
    return lax.ppermute(x, AXES, pairs)


def across(x, reach):
    return permuted(x, lambda i: i ^ reach)


def within_parity(x, reach, sign):
    return permuted(x, lambda i: i + (sign if i & reach else -sign) * 2 * reach)


def dot(a, b):
    return jnp.dot(a, b, preferred_element_type=F32)


def dot_t(a, b):
    return lax.dot_general(a, b, (((1,), (1,)), ((), ())), preferred_element_type=F32)


def contract_rows(a, b):
    return lax.dot_general(a, b, (((0,), (0,)), ((), ())), preferred_element_type=F32)


def gelu_terms(v):
    slope = 0.7978845608028654
    t = jnp.tanh(slope * (v + 0.044715 * (v * v * v)))
    half = 0.5 * (1.0 + t)
    value = v * half
    derivative = half + 0.5 * v * (1.0 - t * t) * (slope * (1.0 + 0.134145 * (v * v)))
    return value, derivative


def row_block(width, first=0):
    return pl.BlockSpec((TILE, width), lambda i, s: (i + first, 0))


def tap(place):
    return pl.BlockSpec((D, H), lambda i, s: (s[place], 0))


CENTER = pl.BlockSpec((D, H), lambda i, s: (1, 0))
WHOLE = pl.BlockSpec((D, H), lambda i, s: (0, 0))
ANYWHERE = pl.BlockSpec(memory_space=pl.ANY)
IN_VMEM = pl.BlockSpec(memory_space=pltpu.VMEM)

SHORT = pl.CostEstimate(flops=1, bytes_accessed=1, transcendentals=0)


def into_rows(body, scalars, chunk, rows, operands, name, previous):
    n = len(operands)
    tiles = rows // CHUNKS // TILE

    def wrapped(s, *refs):
        body(s, *refs[:n], refs[-1])

    whole = pl.pallas_call(
        wrapped,
        out_shape=jax.ShapeDtypeStruct((rows, D), BF16),
        grid_spec=pltpu.PrefetchScalarGridSpec(
            num_scalar_prefetch=1,
            grid=(tiles,),
            in_specs=[spec for _, spec in operands] + [ANYWHERE] * len(previous),
            out_specs=row_block(D, chunk * tiles),
        ),
        cost_estimate=SHORT,
        compiler_params=pltpu.CompilerParams(vmem_limit_bytes=12 * 2**20),
        input_output_aliases={1 + n: 0} if previous else {},
        name=name,
    )(scalars, *[a for a, _ in operands], *previous)
    return [whole]


def resident(body, name, scalars, operands, outs, after=(), vmem=8, kind=BF16):
    n = len(operands)

    def wrapped(s, *refs):
        body(s, *refs[:n], *refs[n + len(after) :])

    return pl.pallas_call(
        wrapped,
        out_shape=[jax.ShapeDtypeStruct(shape, kind) for shape in outs],
        in_specs=[pl.BlockSpec(memory_space=pltpu.SMEM)] + [IN_VMEM] * n + [ANYWHERE] * len(after),
        out_specs=[IN_VMEM] * len(outs),
        cost_estimate=SHORT,
        compiler_params=pltpu.CompilerParams(vmem_limit_bytes=vmem * 2**20),
        name=name,
    )(scalars, *operands, *after)


def tap_of(s, weight, place):
    return weight[pl.ds(pl.multiple_of(s[place] * D, D), D), :]


def center_of(weight):
    return weight[D : 2 * D, :]


def tiles_of(ref):
    return [slice(i, i + TILE) for i in range(0, ref.shape[0], TILE)]


def from_row(first, rows):
    return slice(first + rows.start, first + rows.stop)


def first_product(s, x, w_far, *refs):
    refs[-1][...] = dot(x[...], w_far[...]).astype(BF16)


def near_sum(s, x, weight, arrived, total, place, first=0):
    w = tap_of(s, weight, place)
    for r in tiles_of(total):
        total[r] = (dot(x[from_row(first, r)], w) + arrived[r].astype(F32)).astype(BF16)


def first_block(s, x, crossed, w1, proj, w2, mid, inner, slope, sent, first):
    w_center, w_far2 = center_of(w1), tap_of(s, w2, FAR2)
    for r in tiles_of(mid):
        rows = x[from_row(first, r)]
        value, derivative = gelu_terms(dot(rows, w_center) + crossed[r].astype(F32))
        slope[r] = derivative.astype(BF16)
        value = value.astype(BF16)
        inner[r] = value
        result = (rows.astype(F32) + dot_t(value, proj[...])).astype(BF16)
        mid[r] = result
        sent[r] = dot(result, w_far2).astype(BF16)


def second_block(s, mid, crossed, w2, g, proj, own, inner, first):
    w_center = center_of(w2)
    for r in tiles_of(mid):
        value, derivative = gelu_terms(dot(mid[r], w_center) + crossed[r].astype(F32))
        inner[r] = value.astype(BF16)
        own[r] = (derivative * dot(g[from_row(first, r)], proj[...])).astype(BF16)


def input_gradient(g, own, near, far, w_center, w_near, w_far):
    return (
        g.astype(F32) + dot_t(own, w_center) + dot_t(near, w_near) + dot_t(far, w_far)
    ).astype(BF16)


def middle_gradient(s, g, own, near, far, w2, proj, slope, gmid, own1, first):
    taps = center_of(w2), tap_of(s, w2, NEAR2), tap_of(s, w2, FAR2)
    for r in tiles_of(gmid):
        result = input_gradient(g[from_row(first, r)], own[r], near[r], far[r], *taps)
        gmid[r] = result
        own1[r] = (slope[r].astype(F32) * dot(result, proj[...])).astype(BF16)


def output_rows(s, mid, inner2, proj, out):
    out[...] = (mid[...].astype(F32) + dot_t(inner2[...], proj[...])).astype(BF16)


def gradient_rows(s, gmid, own, near, far, w_center, w_near, w_far, gx):
    gx[...] = input_gradient(
        gmid[...], own[...], near[...], far[...], w_center[...], w_near[...], w_far[...]
    )


def place_rows(s, total, targets, before, block_rows, unit_of, row_in_block):
    for i in range(total.shape[0] // UNIT):
        block, offset = unit_of(i)
        row = (block // 2) * block_rows + row_in_block + offset * UNIT
        row = row if isinstance(row, int) else pl.multiple_of(row, UNIT)
        piece = total[i * UNIT : (i + 1) * UNIT]
        rows = pl.ds(row, UNIT)
        for other in range(2):
            target, earlier = targets[other], before[other : other + 1]

            @pl.when(block % 2 == (1 - s[CORE] if other else s[CORE]))
            def _():
                value = sum((e[rows, :] for e in earlier), piece)
                target[rows, :] = value.astype(target.dtype)


def kernel_gradient(s, x, first, own, near, far, near_place, far_place, targets, before, block_rows):
    around = jnp.concatenate([own[...], near[...], far[...]], 1)
    for half in range(2):
        left = x[first : first + own.shape[0], half * 384 : half * 384 + 384]
        total = contract_rows(left, around)
        for j, k in enumerate((1, s[near_place], s[far_place])):

            def unit_of(i, k=k, half=half):
                u = k * 16 + half * 8 + i
                return u // 3, u % 3

            place_rows(
                s, total[:, j * H : (j + 1) * H], targets, before, block_rows, unit_of, 0
            )


def early_gradients(s, g, mid, own, near, far, inner2, gmid, inner1, *refs, first):
    before, targets = refs[:-2], refs[-2:]
    kernel_gradient(s, mid, 0, own, near, far, NEAR2, FAR2, targets, before, 240)
    for left, begin, right, first_row in ((g, first, inner2, 144), (gmid, 0, inner1, 192)):
        for half in range(2):
            columns = left[begin : begin + right.shape[0], half * 384 : half * 384 + 384]
            place_rows(
                s,
                contract_rows(columns, right[...]),
                targets,
                before,
                240,
                lambda i, half=half: (half * 8 + i, 0),
                first_row,
            )


def late_gradients(s, x, own, near, far, *refs, first):
    kernel_gradient(s, x, first, own, near, far, NEAR1, FAR1, refs[-2:], refs[:-2], 144)


def add_pair(s, kept, arrived, *pieces):
    rows = pieces[0].shape[0]
    for j, piece in enumerate(pieces):
        place = pl.ds(pl.multiple_of((s[PLANE] ^ j) * rows, UNIT), rows)
        piece[...] = (kept[place, :].astype(F32) + arrived[place, :].astype(F32)).astype(BF16)


def plane_pieces(scalars, kept, given, name):
    arrived = across(given, 16)
    pieces = resident(add_pair, name, scalars, [kept, arrived], [(kept.shape[0] // 8, H)] * 8)
    return [pieces[0]] + [across(pieces[j], 32 * j) for j in PIECE_ORDER]


def plane_exchange(kept, given):
    arrived = across(given, 16)
    pair = (kept.astype(F32) + arrived.astype(F32)).astype(BF16)
    return lax.all_to_all(pair, ("y", "x_lo"), 0, 0, tiled=True), pair


def sum_pieces(pieces):
    return sum(p[...].astype(F32) for p in pieces)


def arrange_lines(*refs):
    early, late, lines = refs[0], refs[1:9], refs[-1]
    early_rows = sum_pieces(early.at[pl.ds(240 * i, 240)] for i in range(8))
    late_rows = sum_pieces(late)
    for i in range(16):
        lines[i, 0:9] = early_rows[9 * i : 9 * i + 9].astype(BF16)
        lines[i, 9:18] = late_rows[9 * i : 9 * i + 9].astype(BF16)
        lines[i, 18:21] = early_rows[144 + 3 * i : 147 + 3 * i].astype(BF16)
        lines[i, 21:24] = early_rows[192 + 3 * i : 195 + 3 * i].astype(BF16)


def finish(lines, kernel2, kernel1, point2, point1):
    done = jnp.sum(lines[...].astype(F32), 0)
    kernel2[...] = done[0:9]
    kernel1[...] = done[9:18]
    point2[...] = done[18:21]
    point1[...] = done[21:24]


def per_device(x, cotangent, w1, p1, w2, p2):
    index = lax.axis_index(AXES)
    core = lax.axis_index("core")
    rows = x.shape[0]
    reach1, reach2 = FIRST_SPACING // rows, SECOND_SPACING // rows
    odd1, odd2 = (index // reach1) % 2, (index // reach2) % 2
    scalars = jnp.stack([2 - 2 * odd1, 2 * odd1, 2 - 2 * odd2, 2 * odd2, core, index // 32]).astype(
        jnp.int32
    )
    size = rows // CHUNKS
    narrow, wide = (size, H), (size, D)
    chunks, output, gx, early, late = [], [], [], [], []
    for c in range(CHUNKS):
        here = functools.partial(functools.partial, first=c * size)
        def turn(name):
            return [chunks[-1][name]] if chunks else []

        sent = pl.pallas_call(
            first_product,
            out_shape=jax.ShapeDtypeStruct(narrow, BF16),
            grid_spec=pltpu.PrefetchScalarGridSpec(
                num_scalar_prefetch=1,
                grid=(size // TILE,),
                in_specs=[row_block(D, c * (size // TILE)), tap(FAR1)] + [ANYWHERE] * len(turn("arrived1")),
                out_specs=row_block(H),
            ),
            cost_estimate=SHORT,
            compiler_params=pltpu.CompilerParams(vmem_limit_bytes=24 * 2**20),
            name="first_product",
        )(scalars, x, w1, *turn("arrived1"))
        arrived1 = arrived = within_parity(sent, reach1, 1)
        (total,) = resident(
            here(near_sum, place=NEAR1),
            "first_near_sum",
            scalars,
            [x, w1, arrived],
            [narrow],
            after=turn("crossed1"),
        )
        crossed1 = crossed = across(total, reach1)
        mid, inner1, slope1, sent = resident(
            here(first_block), "first_block", scalars, [x, crossed, w1, p1, w2], [wide] + [narrow] * 3,
            after=turn("total2"),
        )
        arrived = within_parity(sent, reach2, 1)
        (total,) = resident(
            functools.partial(near_sum, place=NEAR2),
            "second_near_sum",
            scalars,
            [mid, w2, arrived],
            [narrow],
            after=turn("own2"),
        )
        total2 = total
        crossed = across(total, reach2)
        own2, inner2 = resident(
            here(second_block), "second_block", scalars, [mid, crossed, w2, cotangent, p2], [narrow] * 2,
            after=turn("near2"),
        )
        output = into_rows(
            output_rows,
            scalars,
            c,
            rows,
            [(mid, row_block(D)), (inner2, row_block(H)), (p2, WHOLE)],
            "output_rows",
            output,
        )
        near2 = across(own2, reach2)
        far2 = within_parity(near2, reach2, -1)
        gmid, own1 = resident(
            here(middle_gradient),
            "middle_gradient",
            scalars,
            [cotangent, own2, near2, far2, w2, p1, slope1],
            [wide, narrow],
            after=turn("near1") + ([early[0]] + output if c == CHUNKS - 1 else []),
        )
        near1 = across(own1, reach1)
        far1 = within_parity(near1, reach1, -1)
        last = c == CHUNKS - 1
        early = resident(
            here(early_gradients),
            "early_gradients",
            scalars,
            [cotangent, mid, own2, near2, far2, inner2, gmid, inner1, *early],
            [(8 * 240, H)] * 2,
            vmem=12,
            kind=BF16 if last else F32,
        )
        chunks.append(
            dict(
                arrived1=arrived1, crossed1=crossed1, total2=total2, mid=mid, inner1=inner1, inner2=inner2, gmid=gmid,
                own1=own1, near1=near1, far1=far1, own2=own2, near2=near2, far2=far2,
            )
        )

    early, early_pair = plane_exchange(*early)
    for c, chunk in enumerate(chunks):
        last = c == CHUNKS - 1
        around = [chunk[name] for name in ("own1", "near1", "far1")]
        late = resident(
            functools.partial(late_gradients, first=c * size),
            "late_gradients",
            scalars,
            [x, *around, *late],
            [(8 * 144, H)] * 2,
            after=[early_pair] if last else [],
            vmem=12,
            kind=BF16 if last else F32,
        )
        gx = into_rows(
            gradient_rows,
            scalars,
            c,
            rows,
            [(chunk["gmid"], row_block(D))]
            + [(a, row_block(H)) for a in around]
            + [(w1, CENTER), (w1, tap(NEAR1)), (w1, tap(FAR1))],
            "gradient_rows",
            gx,
        )
    late = plane_pieces(scalars, *late, "late_pair")
    lines = pl.pallas_call(
        arrange_lines,
        out_shape=jax.ShapeDtypeStruct((16, 24, H), BF16),
        in_specs=[IN_VMEM] * 9 + [ANYWHERE],
        out_specs=IN_VMEM,
        cost_estimate=SHORT,
        name="arrange_lines",
    )(early, *late, gx[0])
    lines = lax.all_to_all(lines, ("x_hi", "z"), 0, 0, tiled=True)
    kernel2, kernel1, point2, point1 = pl.pallas_call(
        finish,
        out_shape=[jax.ShapeDtypeStruct((n, H), F32) for n in (9, 9, 3, 3)],
        in_specs=[IN_VMEM],
        out_specs=[IN_VMEM] * 4,
        cost_estimate=SHORT,
        name="finish",
    )(lines)
    return (output[0], gx[0], kernel1, point1, kernel2, point2)


def solution(mesh):
    fine = Mesh(mesh.devices.reshape(FINE_SHAPE), AXES)
    placed = P(AXES, None)
    return jax.shard_map(
        per_device,
        mesh=fine,
        in_specs=(placed, placed, P(), P(), P(), P()),
        out_specs=(placed,) * 6,
        check_vma=False,
    )
```

```python
import functools

import jax
import jax.numpy as jnp
from jax import lax
from jax.experimental import pallas as pl
from jax.experimental.pallas import tpu as pltpu
from jax.sharding import Mesh
from jax.sharding import PartitionSpec as P

AXES = ("y", "x_lo", "core", "x_hi", "z")
FINE_SHAPE = (4, 2, 2, 2, 8)
DEVICES = 256
FIRST_SPACING = 4096
SECOND_SPACING = 8192
CHUNKS = 2
TILE = 256
D = 768
H = 384
PIECE_ORDER = (4, 5, 6, 7, 2, 3, 1)
UNIT = 48
F32 = jnp.float32
BF16 = jnp.bfloat16
FAR1, NEAR1, FAR2, NEAR2, CORE, PLANE = range(6)


def permuted(x, target):
    pairs = [(i, target(i)) for i in range(DEVICES) if 0 <= target(i) < DEVICES]
    return lax.ppermute(x, AXES, pairs)


def across(x, reach):
    return permuted(x, lambda i: i ^ reach)


def within_parity(x, reach, sign):
    return permuted(x, lambda i: i + (sign if i & reach else -sign) * 2 * reach)


def dot(a, b):
    return jnp.dot(a, b, preferred_element_type=F32)


def dot_t(a, b):
    return lax.dot_general(a, b, (((1,), (1,)), ((), ())), preferred_element_type=F32)


def contract_rows(a, b):
    return lax.dot_general(a, b, (((0,), (0,)), ((), ())), preferred_element_type=F32)


def gelu_terms(v):
    slope = 0.7978845608028654
    t = jnp.tanh(slope * (v + 0.044715 * (v * v * v)))
    half = 0.5 * (1.0 + t)
    value = v * half
    derivative = half + 0.5 * v * (1.0 - t * t) * (slope * (1.0 + 0.134145 * (v * v)))
    return value, derivative


def row_block(width, first=0):
    return pl.BlockSpec((TILE, width), lambda i, s: (i + first, 0))


def tap(place):
    return pl.BlockSpec((D, H), lambda i, s: (s[place], 0))


CENTER = pl.BlockSpec((D, H), lambda i, s: (1, 0))
WHOLE = pl.BlockSpec((D, H), lambda i, s: (0, 0))
ANYWHERE = pl.BlockSpec(memory_space=pl.ANY)
IN_VMEM = pl.BlockSpec(memory_space=pltpu.VMEM)

SHORT = pl.CostEstimate(flops=1, bytes_accessed=1, transcendentals=0)


def into_rows(body, scalars, chunk, rows, operands, name, previous, after=()):
    n = len(operands)
    tiles = rows // CHUNKS // TILE

    def wrapped(s, *refs):
        body(s, *refs[:n], refs[-1])

    whole = pl.pallas_call(
        wrapped,
        out_shape=jax.ShapeDtypeStruct((rows, D), BF16),
        grid_spec=pltpu.PrefetchScalarGridSpec(
            num_scalar_prefetch=1,
            grid=(tiles,),
            in_specs=[spec for _, spec in operands] + [ANYWHERE] * (len(previous) + len(after)),
            out_specs=row_block(D, chunk * tiles),
        ),
        cost_estimate=SHORT,
        compiler_params=pltpu.CompilerParams(vmem_limit_bytes=12 * 2**20),
        input_output_aliases={1 + n: 0} if previous else {},
        name=name,
    )(scalars, *[a for a, _ in operands], *previous, *after)
    return [whole]


def resident(body, name, scalars, operands, outs, after=(), vmem=8, kind=BF16):
    n = len(operands)

    def wrapped(s, *refs):
        body(s, *refs[:n], *refs[n + len(after) :])

    return pl.pallas_call(
        wrapped,
        out_shape=[jax.ShapeDtypeStruct(shape, kind) for shape in outs],
        in_specs=[pl.BlockSpec(memory_space=pltpu.SMEM)] + [IN_VMEM] * n + [ANYWHERE] * len(after),
        out_specs=[IN_VMEM] * len(outs),
        cost_estimate=SHORT,
        compiler_params=pltpu.CompilerParams(vmem_limit_bytes=vmem * 2**20),
        name=name,
    )(scalars, *operands, *after)


def tap_of(s, weight, place):
    return weight[pl.ds(pl.multiple_of(s[place] * D, D), D), :]


def center_of(weight):
    return weight[D : 2 * D, :]


def tiles_of(ref):
    return [slice(i, i + TILE) for i in range(0, ref.shape[0], TILE)]


def from_row(first, rows):
    return slice(first + rows.start, first + rows.stop)


def first_product(s, x, w_far, *refs):
    refs[-1][...] = dot(x[...], w_far[...]).astype(BF16)


def near_sum(s, x, weight, arrived, total, place, first=0):
    w = tap_of(s, weight, place)
    for r in tiles_of(total):
        total[r] = (dot(x[from_row(first, r)], w) + arrived[r].astype(F32)).astype(BF16)


def first_block(s, x, crossed, w1, proj, w2, mid, inner, slope, sent, first):
    w_center, w_far2 = center_of(w1), tap_of(s, w2, FAR2)
    for r in tiles_of(mid):
        rows = x[from_row(first, r)]
        value, derivative = gelu_terms(dot(rows, w_center) + crossed[r].astype(F32))
        slope[r] = derivative.astype(BF16)
        value = value.astype(BF16)
        inner[r] = value
        result = (rows.astype(F32) + dot_t(value, proj[...])).astype(BF16)
        mid[r] = result
        sent[r] = dot(result, w_far2).astype(BF16)


def second_block(s, mid, crossed, w2, g, proj, own, inner, first):
    w_center = center_of(w2)
    for r in tiles_of(mid):
        value, derivative = gelu_terms(dot(mid[r], w_center) + crossed[r].astype(F32))
        inner[r] = value.astype(BF16)
        own[r] = (derivative * dot(g[from_row(first, r)], proj[...])).astype(BF16)


def input_gradient(g, own, near, far, w_center, w_near, w_far):
    return (
        g.astype(F32) + dot_t(own, w_center) + dot_t(near, w_near) + dot_t(far, w_far)
    ).astype(BF16)


def middle_gradient(s, g, own, near, far, w2, proj, slope, gmid, own1, first):
    taps = center_of(w2), tap_of(s, w2, NEAR2), tap_of(s, w2, FAR2)
    for r in tiles_of(gmid):
        result = input_gradient(g[from_row(first, r)], own[r], near[r], far[r], *taps)
        gmid[r] = result
        own1[r] = (slope[r].astype(F32) * dot(result, proj[...])).astype(BF16)


def output_rows(s, mid, inner2, proj, out):
    out[...] = (mid[...].astype(F32) + dot_t(inner2[...], proj[...])).astype(BF16)


def gradient_rows(s, gmid, own, near, far, w_center, w_near, w_far, gx):
    gx[...] = input_gradient(
        gmid[...], own[...], near[...], far[...], w_center[...], w_near[...], w_far[...]
    )


def place_rows(s, total, targets, before, block_rows, unit_of, row_in_block):
    for i in range(total.shape[0] // UNIT):
        block, offset = unit_of(i)
        row = (block // 2) * block_rows + row_in_block + offset * UNIT
        row = row if isinstance(row, int) else pl.multiple_of(row, UNIT)
        piece = total[i * UNIT : (i + 1) * UNIT]
        rows = pl.ds(row, UNIT)
        for other in range(2):
            target, earlier = targets[other], before[other : other + 1]

            @pl.when(block % 2 == (1 - s[CORE] if other else s[CORE]))
            def _():
                value = sum((e[rows, :] for e in earlier), piece)
                target[rows, :] = value.astype(target.dtype)


def kernel_gradient(s, x, first, own, near, far, near_place, far_place, targets, before, block_rows):
    around = jnp.concatenate([own[...], near[...], far[...]], 1)
    for half in range(2):
        left = x[first : first + own.shape[0], half * 384 : half * 384 + 384]
        total = contract_rows(left, around)
        for j, k in enumerate((1, s[near_place], s[far_place])):

            def unit_of(i, k=k, half=half):
                u = k * 16 + half * 8 + i
                return u // 3, u % 3

            place_rows(
                s, total[:, j * H : (j + 1) * H], targets, before, block_rows, unit_of, 0
            )


def early_gradients(s, g, mid, own, near, far, inner2, gmid, inner1, *refs, first):
    before, targets = refs[:-2], refs[-2:]
    kernel_gradient(s, mid, 0, own, near, far, NEAR2, FAR2, targets, before, 240)
    for left, begin, right, first_row in ((g, first, inner2, 144), (gmid, 0, inner1, 192)):
        for half in range(2):
            columns = left[begin : begin + right.shape[0], half * 384 : half * 384 + 384]
            place_rows(
                s,
                contract_rows(columns, right[...]),
                targets,
                before,
                240,
                lambda i, half=half: (half * 8 + i, 0),
                first_row,
            )


def late_gradients(s, x, own, near, far, *refs, first):
    kernel_gradient(s, x, first, own, near, far, NEAR1, FAR1, refs[-2:], refs[:-2], 144)


def add_pair(s, kept, arrived, *pieces):
    rows = pieces[0].shape[0]
    for j, piece in enumerate(pieces):
        place = pl.ds(pl.multiple_of((s[PLANE] ^ j) * rows, UNIT), rows)
        piece[...] = (kept[place, :].astype(F32) + arrived[place, :].astype(F32)).astype(BF16)


def plane_pieces(scalars, kept, given, name):
    arrived = across(given, 16)
    pieces = resident(add_pair, name, scalars, [kept, arrived], [(kept.shape[0] // 8, H)] * 8)
    return [pieces[0]] + [across(pieces[j], 32 * j) for j in PIECE_ORDER]


def plane_exchange(kept, given):
    arrived = across(given, 16)
    pair = (kept.astype(F32) + arrived.astype(F32)).astype(BF16)
    return lax.all_to_all(pair, ("y", "x_lo"), 0, 0, tiled=True), pair


def sum_pieces(pieces):
    return sum(p[...].astype(F32) for p in pieces)


def add_early(s, pieces, rows):
    rows[...] = sum_pieces(pieces.at[pl.ds(240 * i, 240)] for i in range(8)).astype(BF16)


def arrange_lines(s, early, *refs):
    late, lines = sum_pieces(refs[:8]).astype(BF16), refs[-1]
    for i in range(16):
        lines[i, 0:9] = early[9 * i : 9 * i + 9]
        lines[i, 9:18] = late[9 * i : 9 * i + 9]
        lines[i, 18:21] = early[144 + 3 * i : 147 + 3 * i]
        lines[i, 21:24] = early[192 + 3 * i : 195 + 3 * i]


def finish(lines, kernel2, kernel1, point2, point1):
    done = jnp.sum(lines[...].astype(F32), 0)
    kernel2[...] = done[0:9]
    kernel1[...] = done[9:18]
    point2[...] = done[18:21]
    point1[...] = done[21:24]


def per_device(x, cotangent, w1, p1, w2, p2):
    index = lax.axis_index(AXES)
    core = lax.axis_index("core")
    rows = x.shape[0]
    reach1, reach2 = FIRST_SPACING // rows, SECOND_SPACING // rows
    odd1, odd2 = (index // reach1) % 2, (index // reach2) % 2
    scalars = jnp.stack([2 - 2 * odd1, 2 * odd1, 2 - 2 * odd2, 2 * odd2, core, index // 32]).astype(
        jnp.int32
    )
    size = rows // CHUNKS
    narrow, wide = (size, H), (size, D)
    chunks, output, gx, early, late = [], [], [], [], []
    for c in range(CHUNKS):
        here = functools.partial(functools.partial, first=c * size)
        def turn(name):
            return [chunks[-1][name]] if chunks else []

        sent = pl.pallas_call(
            first_product,
            out_shape=jax.ShapeDtypeStruct(narrow, BF16),
            grid_spec=pltpu.PrefetchScalarGridSpec(
                num_scalar_prefetch=1,
                grid=(size // TILE,),
                in_specs=[row_block(D, c * (size // TILE)), tap(FAR1)] + [ANYWHERE] * len(turn("arrived1")),
                out_specs=row_block(H),
            ),
            cost_estimate=SHORT,
            compiler_params=pltpu.CompilerParams(vmem_limit_bytes=24 * 2**20),
            name="first_product",
        )(scalars, x, w1, *turn("arrived1"))
        arrived1 = arrived = within_parity(sent, reach1, 1)
        (total,) = resident(
            here(near_sum, place=NEAR1),
            "first_near_sum",
            scalars,
            [x, w1, arrived],
            [narrow],
            after=turn("crossed1"),
        )
        crossed1 = crossed = across(total, reach1)
        mid, inner1, slope1, sent = resident(
            here(first_block), "first_block", scalars, [x, crossed, w1, p1, w2], [wide] + [narrow] * 3,
            after=turn("total2"),
        )
        arrived = within_parity(sent, reach2, 1)
        (total,) = resident(
            functools.partial(near_sum, place=NEAR2),
            "second_near_sum",
            scalars,
            [mid, w2, arrived],
            [narrow],
            after=turn("own2"),
        )
        total2 = total
        crossed = across(total, reach2)
        own2, inner2 = resident(
            here(second_block), "second_block", scalars, [mid, crossed, w2, cotangent, p2], [narrow] * 2,
            after=turn("near2"),
        )
        output = into_rows(
            output_rows,
            scalars,
            c,
            rows,
            [(mid, row_block(D)), (inner2, row_block(H)), (p2, WHOLE)],
            "output_rows",
            output,
        )
        near2 = across(own2, reach2)
        far2 = within_parity(near2, reach2, -1)
        gmid, own1 = resident(
            here(middle_gradient),
            "middle_gradient",
            scalars,
            [cotangent, own2, near2, far2, w2, p1, slope1],
            [wide, narrow],
            after=turn("near1") + ([early[0]] + output if c == CHUNKS - 1 else []),
        )
        near1 = across(own1, reach1)
        far1 = within_parity(near1, reach1, -1)
        last = c == CHUNKS - 1
        early = resident(
            here(early_gradients),
            "early_gradients",
            scalars,
            [cotangent, mid, own2, near2, far2, inner2, gmid, inner1, *early],
            [(8 * 240, H)] * 2,
            vmem=12,
            kind=BF16 if last else F32,
        )
        chunks.append(
            dict(
                arrived1=arrived1, crossed1=crossed1, total2=total2, mid=mid, inner1=inner1, inner2=inner2, gmid=gmid,
                own1=own1, near1=near1, far1=far1, own2=own2, near2=near2, far2=far2,
            )
        )

    early, early_pair = plane_exchange(*early)
    for c, chunk in enumerate(chunks):
        last = c == CHUNKS - 1
        around = [chunk[name] for name in ("own1", "near1", "far1")]
        late = resident(
            functools.partial(late_gradients, first=c * size),
            "late_gradients",
            scalars,
            [x, *around, *late],
            [(8 * 144, H)] * 2,
            after=[early_pair] if last else [],
            vmem=12,
            kind=BF16 if last else F32,
        )
    late = plane_pieces(scalars, *late, "late_pair")
    early_rows = resident(add_early, "early_rows", scalars, [early], [(240, H)])
    for c, chunk in enumerate(chunks):
        if c == CHUNKS - 1:
            (lines,) = resident(
                arrange_lines, "lines", scalars, [*early_rows, *late], [(16, 24, H)], after=gx
            )
        gx = into_rows(
            gradient_rows,
            scalars,
            c,
            rows,
            [(chunk["gmid"], row_block(D))]
            + [(a, row_block(H)) for a in (chunk["own1"], chunk["near1"], chunk["far1"])]
            + [(w1, CENTER), (w1, tap(NEAR1)), (w1, tap(FAR1))],
            "gradient_rows",
            gx,
            after=early_rows if c == 0 else [],
        )
    lines = lax.all_to_all(lines, ("x_hi", "z"), 0, 0, tiled=True)
    kernel2, kernel1, point2, point1 = pl.pallas_call(
        finish,
        out_shape=[jax.ShapeDtypeStruct((n, H), F32) for n in (9, 9, 3, 3)],
        in_specs=[IN_VMEM],
        out_specs=[IN_VMEM] * 4,
        cost_estimate=SHORT,
        name="finish",
    )(lines)
    return (output[0], gx[0], kernel1, point1, kernel2, point2)


def solution(mesh):
    fine = Mesh(mesh.devices.reshape(FINE_SHAPE), AXES)
    placed = P(AXES, None)
    return jax.shard_map(
        per_device,
        mesh=fine,
        in_specs=(placed, placed, P(), P(), P(), P()),
        out_specs=(placed,) * 6,
        check_vma=False,
    )
```

```python
import functools

import jax
import jax.numpy as jnp
from jax import lax
from jax.experimental import pallas as pl
from jax.experimental.pallas import tpu as pltpu
from jax.sharding import Mesh
from jax.sharding import PartitionSpec as P

AXES = ("y", "x_lo", "core", "x_hi", "z")
FINE_SHAPE = (4, 2, 2, 2, 8)
DEVICES = 256
FIRST_SPACING = 4096
SECOND_SPACING = 8192
CHUNKS = 2
TILE = 256
D = 768
H = 384
PIECE_ORDER = (4, 5, 6, 7, 2, 3, 1)
UNIT = 48
F32 = jnp.float32
BF16 = jnp.bfloat16
FAR1, NEAR1, CORE, PLANE = range(4)


def permuted(x, target):
    pairs = [(i, target(i)) for i in range(DEVICES) if 0 <= target(i) < DEVICES]
    return lax.ppermute(x, AXES, pairs)


def across(x, reach):
    return permuted(x, lambda i: i ^ reach)


def moved(x, by):
    return permuted(x, lambda i: i + by)


def within_parity(x, reach, sign):
    return permuted(x, lambda i: i + (sign if i & reach else -sign) * 2 * reach)


def dot(a, b):
    return jnp.dot(a, b, preferred_element_type=F32)


def dot_t(a, b):
    return lax.dot_general(a, b, (((1,), (1,)), ((), ())), preferred_element_type=F32)


def contract_rows(a, b):
    return lax.dot_general(a, b, (((0,), (0,)), ((), ())), preferred_element_type=F32)


def gelu_terms(v):
    slope = 0.7978845608028654
    t = jnp.tanh(slope * (v + 0.044715 * (v * v * v)))
    half = 0.5 * (1.0 + t)
    value = v * half
    derivative = half + 0.5 * v * (1.0 - t * t) * (slope * (1.0 + 0.134145 * (v * v)))
    return value, derivative


def row_block(width, first=0):
    return pl.BlockSpec((TILE, width), lambda i, s: (i + first, 0))


def tap(place):
    return pl.BlockSpec((D, H), lambda i, s: (s[place], 0))


CENTER = pl.BlockSpec((D, H), lambda i, s: (1, 0))
WHOLE = pl.BlockSpec((D, H), lambda i, s: (0, 0))
ANYWHERE = pl.BlockSpec(memory_space=pl.ANY)
IN_VMEM = pl.BlockSpec(memory_space=pltpu.VMEM)

SHORT = pl.CostEstimate(flops=1, bytes_accessed=1, transcendentals=0)


def into_rows(body, scalars, chunk, rows, operands, name, previous):
    n = len(operands)
    tiles = rows // CHUNKS // TILE

    def wrapped(s, *refs):
        body(s, *refs[:n], refs[-1])

    whole = pl.pallas_call(
        wrapped,
        out_shape=jax.ShapeDtypeStruct((rows, D), BF16),
        grid_spec=pltpu.PrefetchScalarGridSpec(
            num_scalar_prefetch=1,
            grid=(tiles,),
            in_specs=[spec for _, spec in operands] + [ANYWHERE] * len(previous),
            out_specs=row_block(D, chunk * tiles),
        ),
        cost_estimate=SHORT,
        compiler_params=pltpu.CompilerParams(vmem_limit_bytes=12 * 2**20),
        input_output_aliases={1 + n: 0} if previous else {},
        name=name,
    )(scalars, *[a for a, _ in operands], *previous)
    return [whole]


def resident(body, name, scalars, operands, outs, after=(), vmem=8, kind=BF16):
    n = len(operands)

    def wrapped(s, *refs):
        body(s, *refs[:n], *refs[n + len(after) :])

    return pl.pallas_call(
        wrapped,
        out_shape=[jax.ShapeDtypeStruct(shape, kind) for shape in outs],
        in_specs=[pl.BlockSpec(memory_space=pltpu.SMEM)] + [IN_VMEM] * n + [ANYWHERE] * len(after),
        out_specs=[IN_VMEM] * len(outs),
        cost_estimate=SHORT,
        compiler_params=pltpu.CompilerParams(vmem_limit_bytes=vmem * 2**20),
        name=name,
    )(scalars, *operands, *after)


def tap_of(s, weight, place):
    return weight[pl.ds(pl.multiple_of(s[place] * D, D), D), :]


def center_of(weight):
    return weight[D : 2 * D, :]


def tiles_of(ref):
    return [slice(i, i + TILE) for i in range(0, ref.shape[0], TILE)]


def from_row(first, rows):
    return slice(first + rows.start, first + rows.stop)


def first_product(s, x, w_far, *refs):
    refs[-1][...] = dot(x[...], w_far[...]).astype(BF16)


def near_sum(s, x, weight, arrived, total, place, first=0):
    w = tap_of(s, weight, place)
    for r in tiles_of(total):
        total[r] = (dot(x[from_row(first, r)], w) + arrived[r].astype(F32)).astype(BF16)


def first_block(s, x, crossed, w1, proj, w2, mid, inner, slope, up, down, first):
    w_center = center_of(w1)
    for r in tiles_of(mid):
        rows = x[from_row(first, r)]
        value, derivative = gelu_terms(dot(rows, w_center) + crossed[r].astype(F32))
        slope[r] = derivative.astype(BF16)
        value = value.astype(BF16)
        inner[r] = value
        result = (rows.astype(F32) + dot_t(value, proj[...])).astype(BF16)
        mid[r] = result
        up[r] = dot(result, w2[:D, :]).astype(BF16)
        down[r] = dot(result, w2[2 * D :, :]).astype(BF16)


def second_block(s, mid, earlier, later, w2, g, proj, own, inner, first):
    w_center = center_of(w2)
    for r in tiles_of(mid):
        pre = dot(mid[r], w_center) + earlier[r].astype(F32) + later[r].astype(F32)
        value, derivative = gelu_terms(pre)
        inner[r] = value.astype(BF16)
        own[r] = (derivative * dot(g[from_row(first, r)], proj[...])).astype(BF16)


def input_gradient(g, own, near, far, w_center, w_near, w_far):
    return (
        g.astype(F32) + dot_t(own, w_center) + dot_t(near, w_near) + dot_t(far, w_far)
    ).astype(BF16)


def middle_gradient(s, g, own, later, earlier, w2, proj, slope, gmid, own1, first):
    taps = center_of(w2), w2[:D, :], w2[2 * D :, :]
    for r in tiles_of(gmid):
        result = input_gradient(g[from_row(first, r)], own[r], later[r], earlier[r], *taps)
        gmid[r] = result
        own1[r] = (slope[r].astype(F32) * dot(result, proj[...])).astype(BF16)


def output_rows(s, mid, inner2, proj, out):
    out[...] = (mid[...].astype(F32) + dot_t(inner2[...], proj[...])).astype(BF16)


def gradient_rows(s, gmid, own, near, far, w_center, w_near, w_far, gx):
    gx[...] = input_gradient(
        gmid[...], own[...], near[...], far[...], w_center[...], w_near[...], w_far[...]
    )


def place_rows(s, total, targets, before, block_rows, unit_of, row_in_block):
    for i in range(total.shape[0] // UNIT):
        block, offset = unit_of(i)
        row = (block // 2) * block_rows + row_in_block + offset * UNIT
        row = row if isinstance(row, int) else pl.multiple_of(row, UNIT)
        piece = total[i * UNIT : (i + 1) * UNIT]
        rows = pl.ds(row, UNIT)
        for other in range(2):
            target, earlier = targets[other], before[other : other + 1]

            @pl.when(block % 2 == (1 - s[CORE] if other else s[CORE]))
            def _():
                value = sum((e[rows, :] for e in earlier), piece)
                target[rows, :] = value.astype(target.dtype)


def kernel_gradient(s, x, first, own, near, far, taps, targets, before, block_rows):
    around = jnp.concatenate([own[...], near[...], far[...]], 1)
    for half in range(2):
        left = x[first : first + own.shape[0], half * 384 : half * 384 + 384]
        total = contract_rows(left, around)
        for j, k in enumerate((1, *taps)):

            def unit_of(i, k=k, half=half):
                u = k * 16 + half * 8 + i
                return u // 3, u % 3

            place_rows(
                s, total[:, j * H : (j + 1) * H], targets, before, block_rows, unit_of, 0
            )


def early_gradients(s, g, mid, own, near, far, inner2, gmid, inner1, *refs, first):
    before, targets = refs[:-2], refs[-2:]
    kernel_gradient(s, mid, 0, own, near, far, (0, 2), targets, before, 240)
    for left, begin, right, first_row in ((g, first, inner2, 144), (gmid, 0, inner1, 192)):
        for half in range(2):
            columns = left[begin : begin + right.shape[0], half * 384 : half * 384 + 384]
            place_rows(
                s,
                contract_rows(columns, right[...]),
                targets,
                before,
                240,
                lambda i, half=half: (half * 8 + i, 0),
                first_row,
            )


def late_gradients(s, x, own, near, far, *refs, first):
    kernel_gradient(s, x, first, own, near, far, (s[NEAR1], s[FAR1]), refs[-2:], refs[:-2], 144)


def add_pair(s, kept, arrived, *pieces):
    rows = pieces[0].shape[0]
    for j, piece in enumerate(pieces):
        place = pl.ds(pl.multiple_of((s[PLANE] ^ j) * rows, UNIT), rows)
        piece[...] = (kept[place, :].astype(F32) + arrived[place, :].astype(F32)).astype(BF16)


def plane_pieces(scalars, kept, given, name):
    arrived = across(given, 16)
    pieces = resident(add_pair, name, scalars, [kept, arrived], [(kept.shape[0] // 8, H)] * 8)
    return [pieces[0]] + [across(pieces[j], 32 * j) for j in PIECE_ORDER]


def plane_exchange(kept, given):
    arrived = across(given, 16)
    pair = (kept.astype(F32) + arrived.astype(F32)).astype(BF16)
    return lax.all_to_all(pair, ("y", "x_lo"), 0, 0, tiled=True), pair


def sum_pieces(pieces):
    return sum(p[...].astype(F32) for p in pieces)


def arrange_lines(*refs):
    early, late, lines = refs[0], refs[1:9], refs[-1]
    early_rows = sum_pieces(early.at[pl.ds(240 * i, 240)] for i in range(8))
    late_rows = sum_pieces(late)
    for i in range(16):
        lines[i, 0:9] = early_rows[9 * i : 9 * i + 9].astype(BF16)
        lines[i, 9:18] = late_rows[9 * i : 9 * i + 9].astype(BF16)
        lines[i, 18:21] = early_rows[144 + 3 * i : 147 + 3 * i].astype(BF16)
        lines[i, 21:24] = early_rows[192 + 3 * i : 195 + 3 * i].astype(BF16)


def finish(lines, kernel2, kernel1, point2, point1):
    done = jnp.sum(lines[...].astype(F32), 0)
    kernel2[...] = done[0:9]
    kernel1[...] = done[9:18]
    point2[...] = done[18:21]
    point1[...] = done[21:24]


def per_device(x, cotangent, w1, p1, w2, p2):
    index = lax.axis_index(AXES)
    core = lax.axis_index("core")
    rows = x.shape[0]
    reach1, reach2 = FIRST_SPACING // rows, SECOND_SPACING // rows
    odd1 = (index // reach1) % 2
    scalars = jnp.stack([2 - 2 * odd1, 2 * odd1, core, index // 32]).astype(
        jnp.int32
    )
    size = rows // CHUNKS
    narrow, wide = (size, H), (size, D)
    chunks, output, gx, early, late = [], [], [], [], []
    for c in range(CHUNKS):
        here = functools.partial(functools.partial, first=c * size)
        def turn(name):
            return [chunks[-1][name]] if chunks else []

        sent = pl.pallas_call(
            first_product,
            out_shape=jax.ShapeDtypeStruct(narrow, BF16),
            grid_spec=pltpu.PrefetchScalarGridSpec(
                num_scalar_prefetch=1,
                grid=(size // TILE,),
                in_specs=[row_block(D, c * (size // TILE)), tap(FAR1)] + [ANYWHERE] * len(turn("arrived1")),
                out_specs=row_block(H),
            ),
            cost_estimate=SHORT,
            compiler_params=pltpu.CompilerParams(vmem_limit_bytes=24 * 2**20),
            name="first_product",
        )(scalars, x, w1, *turn("arrived1"))
        arrived1 = arrived = within_parity(sent, reach1, 1)
        (total,) = resident(
            here(near_sum, place=NEAR1),
            "first_near_sum",
            scalars,
            [x, w1, arrived],
            [narrow],
            after=turn("crossed1"),
        )
        crossed1 = crossed = across(total, reach1)
        mid, inner1, slope1, up, down = resident(
            here(first_block), "first_block", scalars, [x, crossed, w1, p1, w2], [wide] + [narrow] * 4,
            after=turn("up"),
        )
        earlier, later = moved(up, reach2), moved(down, -reach2)
        own2, inner2 = resident(
            here(second_block), "second_block", scalars, [mid, earlier, later, w2, cotangent, p2], [narrow] * 2,
            after=turn("near2"),
        )
        output = into_rows(
            output_rows,
            scalars,
            c,
            rows,
            [(mid, row_block(D)), (inner2, row_block(H)), (p2, WHOLE)],
            "output_rows",
            output,
        )
        near2, far2 = moved(own2, -reach2), moved(own2, reach2)
        gmid, own1 = resident(
            here(middle_gradient),
            "middle_gradient",
            scalars,
            [cotangent, own2, near2, far2, w2, p1, slope1],
            [wide, narrow],
            after=turn("near1") + ([early[0]] + output if c == CHUNKS - 1 else []),
        )
        near1 = across(own1, reach1)
        far1 = within_parity(near1, reach1, -1)
        last = c == CHUNKS - 1
        early = resident(
            here(early_gradients),
            "early_gradients",
            scalars,
            [cotangent, mid, own2, near2, far2, inner2, gmid, inner1, *early],
            [(8 * 240, H)] * 2,
            vmem=12,
            kind=BF16 if last else F32,
        )
        chunks.append(
            dict(
                arrived1=arrived1, crossed1=crossed1, up=up, mid=mid, inner1=inner1, inner2=inner2, gmid=gmid,
                own1=own1, near1=near1, far1=far1, own2=own2, near2=near2, far2=far2,
            )
        )

    early, early_pair = plane_exchange(*early)
    for c, chunk in enumerate(chunks):
        last = c == CHUNKS - 1
        around = [chunk[name] for name in ("own1", "near1", "far1")]
        late = resident(
            functools.partial(late_gradients, first=c * size),
            "late_gradients",
            scalars,
            [x, *around, *late],
            [(8 * 144, H)] * 2,
            after=[early_pair] if last else [],
            vmem=12,
            kind=BF16 if last else F32,
        )
        gx = into_rows(
            gradient_rows,
            scalars,
            c,
            rows,
            [(chunk["gmid"], row_block(D))]
            + [(a, row_block(H)) for a in around]
            + [(w1, CENTER), (w1, tap(NEAR1)), (w1, tap(FAR1))],
            "gradient_rows",
            gx,
        )
    late = plane_pieces(scalars, *late, "late_pair")
    lines = pl.pallas_call(
        arrange_lines,
        out_shape=jax.ShapeDtypeStruct((16, 24, H), BF16),
        in_specs=[IN_VMEM] * 9 + [ANYWHERE],
        out_specs=IN_VMEM,
        cost_estimate=SHORT,
        name="arrange_lines",
    )(early, *late, gx[0])
    lines = lax.all_to_all(lines, ("x_hi", "z"), 0, 0, tiled=True)
    kernel2, kernel1, point2, point1 = pl.pallas_call(
        finish,
        out_shape=[jax.ShapeDtypeStruct((n, H), F32) for n in (9, 9, 3, 3)],
        in_specs=[IN_VMEM],
        out_specs=[IN_VMEM] * 4,
        cost_estimate=SHORT,
        name="finish",
    )(lines)
    return (output[0], gx[0], kernel1, point1, kernel2, point2)


def solution(mesh):
    fine = Mesh(mesh.devices.reshape(FINE_SHAPE), AXES)
    placed = P(AXES, None)
    return jax.shard_map(
        per_device,
        mesh=fine,
        in_specs=(placed, placed, P(), P(), P(), P()),
        out_specs=(placed,) * 6,
        check_vma=False,
    )
```
